512 devices in a mesh: grp: 32 (over y, x, core), mem: 16 (over z).
Axes of the slice: x: 4, y: 4, z: 16, core: 2. Of those that a mesh axis runs over, the one named last changes fastest.
Arguments:
- tensor_blocks: bfloat16 [4096, 256, 256], P(('grp', 'mem')), may hold values from -6 to 6
- block_coords: int32 [4, 4096], P(None, ('grp', 'mem')), may hold values from 0 to 127, as said below
- live_count: int32 [32, 16], P('grp', 'mem'), may hold values from 6 to 8, as said below
- owner_order: int32 [16, 128], P('mem'), may hold values from 0 to 127, as said below
- factor_two: bfloat16 [16384, 256], P(('grp', 'mem'))
- factor_three: bfloat16 [16384, 256], P(('grp', 'mem'))
- factor_four: bfloat16 [16384, 256], P(('grp', 'mem'))
Outputs:
- new_factor: float32 [16, 2048, 256], P('mem', 'grp')
The draws below stay inside these ranges and needn't reach their ends.
Inputs may be any that keep to these rules, and one draw needn't show every extreme that they name: `block_coords`: rows 1 to 3 lie in 0 to 31. Among one device's live slots, the row-0 entries that fall in one owner's positions (owner g owns positions g * 4 to (g + 1) * 4 - 1 of owner_order[m]) take at most 2 distinct values, and on every device exactly 2 for some owner. `live_count`: some device is full in every draw. `owner_order`: each row is a permutation of 0 to 127.
All inputs are finite; a program needn't handle non-finite values.
Results may differ from the reference program's by a relative error of at most 0.0035.
Values may be sent and summed in bfloat16 or wider, within the bound.
A program may use at most 64 MiB of HBM per device.

```python
import math
import jax
import jax.numpy as jnp
from jax import lax

B = 16
R = 256
NB = 8
RB1_DEV = 4
RB_MEM = 2
CAP = 2
SLAB = 128
RBG = 32
NBLK = 4096
I2 = 16384
N_GRP = 32
N_MEM = 16


def owner_table(key):
    scores = jax.random.randint(key, (N_MEM, SLAB), 0, 1 << 16) * SLAB + jnp.arange(SLAB)[None, :]
    return jnp.argsort(scores, axis=1).astype(jnp.int32)


def draw_owner_order(key, part):
    table = owner_table(key)
    return table


def draw_block_coords(key, part):
    table = owner_table(key)
    key = jax.random.fold_in(key, 23)
    subkeys = jax.random.split(key, 5)
    devices = N_GRP * N_MEM
    member_of = jnp.arange(devices) % N_MEM
    slot_index = jnp.arange(NB)[None, :]
    first_owner = jax.random.randint(subkeys[0], (devices, 1), 0, N_GRP)
    other_owner = jax.random.randint(subkeys[1], (devices, NB), 0, N_GRP)
    owner = jnp.where(slot_index < CAP, first_owner, other_owner)
    picked = jnp.where(slot_index < CAP, slot_index, jax.random.randint(subkeys[2], (devices, NB), 0, CAP))
    scores = jax.random.randint(subkeys[3], (devices, N_GRP, RB1_DEV), 0, 1 << 16) * RB1_DEV + jnp.arange(RB1_DEV)[None, None, :]
    chosen = jnp.argsort(scores, axis=2)[:, :, :CAP]
    chosen_owner = jnp.take_along_axis(chosen, owner[:, :, None], axis=1)
    slot = jnp.take_along_axis(chosen_owner, picked[:, :, None], axis=2)[:, :, 0]
    position = owner * RB1_DEV + slot
    slab_ids = table[member_of[:, None], position]
    others = jax.random.randint(subkeys[4], (3, devices, NB), 0, RBG)
    coords = jnp.concatenate([slab_ids[None], others], axis=0)
    return coords.reshape(4, devices * NB).astype(jnp.int32)


def draw_live_count(key, part):
    key = jax.random.fold_in(key, 37)
    subkeys = jax.random.split(key, 2)
    devices = N_GRP * N_MEM
    counts = jax.random.randint(subkeys[0], (devices,), 3 * NB // 4, NB + 1)
    fullest = jax.random.randint(subkeys[1], (), 0, devices)
    counts = jnp.where(jnp.arange(devices) == fullest, NB, counts)
    return counts.reshape(N_GRP, N_MEM).astype(jnp.int32)


def build_factor(key, noise, spread):
    subkeys = jax.random.split(key, 2)
    position = (jnp.arange(I2) // (RB_MEM * B)).astype(jnp.float32)
    rise = 1.0 + 2.0 * position / max(N_GRP * N_MEM - 1, 1)
    scales = jnp.exp(jax.random.uniform(subkeys[0], (I2,), jnp.float32, 0.0, math.log(spread)))
    shared = jnp.clip(jax.random.normal(subkeys[1], (I2, 1), jnp.float32), -4.0, 4.0)
    values = 0.3 / I2 * (scales * rise)[:, None] * (noise + shared)
    return values.astype(jnp.bfloat16)


def factor_draw(key):
    noise_key, other_key = jax.random.split(key)
    noise = jnp.clip(jax.random.normal(noise_key, (I2, R), jnp.float32), -4.0, 4.0)
    return build_factor(other_key, noise, 10.0)


def draw_factor_two(key, part):
    key = jax.random.fold_in(key, 41)
    return factor_draw(key)


def draw_factor_three(key, part):
    key = jax.random.fold_in(key, 43)
    return factor_draw(key)


def draw_factor_four(key, part):
    key = jax.random.fold_in(key, 47)
    return factor_draw(key)


def level_of(key, shape, cuts, least, largest):
    def one(axis_at, parts):
        draws = jax.random.uniform(jax.random.fold_in(jax.random.fold_in(key, 6), axis_at), (parts,), jnp.float32, least / len(cuts), largest / len(cuts))
        return jnp.repeat(jnp.exp(draws), shape[axis_at] // parts).reshape((-1,) + (1,) * (len(shape) - axis_at - 1))

    gain = one(*cuts[0])
    for cut in cuts[1:]:
        gain = gain * one(*cut)
    return gain


def bell_draw(stream_key, dims, deviation, reach, shards=(), kind=jnp.bfloat16):
    values = jax.random.normal(stream_key, dims, jnp.float32) * deviation
    if len(shards) > 0:
        values = level_of(stream_key, dims, shards, -0.22, 0.18) * values
    return jnp.clip(values, min=-reach, max=reach).astype(kind)


def setup_inputs(seed: int = 0) -> dict:
    seeds = jax.random.split(jax.random.key(seed), 8)
    return {
        "tensor_blocks": bell_draw(seeds[0], (NBLK, B * B, B * B), 1.0, 6.0, ((0, 512),)),
        "block_coords": draw_block_coords(jax.random.fold_in(seeds[7], 71), 0),
        "live_count": draw_live_count(jax.random.fold_in(seeds[7], 71), 0),
        "owner_order": draw_owner_order(jax.random.fold_in(seeds[7], 71), 0),
        "factor_two": draw_factor_two(jax.random.fold_in(seeds[7], 71), 0),
        "factor_three": draw_factor_three(jax.random.fold_in(seeds[7], 71), 0),
        "factor_four": draw_factor_four(jax.random.fold_in(seeds[7], 71), 0),
    }


def gram_matrix(factor):
    return lax.dot_general(factor, factor, (((0,), (0,)), ((), ())), preferred_element_type=jnp.float32)

def cholesky_lower(system):
    size = system.shape[0]
    index = jnp.arange(size, dtype=jnp.int32)

    def column(step, lower):
        row_now = lax.dynamic_index_in_dim(lower, step, 0, keepdims=False)
        target = lax.dynamic_index_in_dim(system, step, 1, keepdims=False)
        corner = lax.dynamic_index_in_dim(target, step, 0, keepdims=False)
        pivot = jnp.sqrt(corner - jnp.dot(row_now, row_now, precision=lax.Precision.HIGHEST))
        values = (target - jnp.dot(lower, row_now, precision=lax.Precision.HIGHEST)) / pivot
        values = jnp.where(index > step, values, jnp.where(index == step, pivot, jnp.zeros_like(values)))
        return lax.dynamic_update_index_in_dim(lower, values[:, None], step, 1)
    return lax.fori_loop(jnp.int32(0), jnp.int32(size), column, jnp.zeros_like(system))

def solve_rows(system, sums):
    lower = cholesky_lower(system)
    size = system.shape[0]

    def forward(step, solved):
        row_now = lax.dynamic_index_in_dim(lower, step, 0, keepdims=False)
        pivot = lax.dynamic_index_in_dim(row_now, step, 0, keepdims=False)
        given = lax.dynamic_index_in_dim(sums, step, 1, keepdims=False)
        values = (given - jnp.dot(solved, row_now, precision=lax.Precision.HIGHEST)) / pivot
        return lax.dynamic_update_index_in_dim(solved, values[:, None], step, 1)
    middle = lax.fori_loop(jnp.int32(0), jnp.int32(size), forward, jnp.zeros_like(sums))

    def backward(count, solved):
        step = (size - 1 - count).astype(jnp.int32)
        col_now = lax.dynamic_index_in_dim(lower, step, 1, keepdims=False)
        pivot = lax.dynamic_index_in_dim(col_now, step, 0, keepdims=False)
        given = lax.dynamic_index_in_dim(middle, step, 1, keepdims=False)
        values = (given - jnp.dot(solved, col_now, precision=lax.Precision.HIGHEST)) / pivot
        return lax.dynamic_update_index_in_dim(solved, values[:, None], step, 1)
    return lax.fori_loop(jnp.int32(0), jnp.int32(size), backward, jnp.zeros_like(sums))

def block_partial(values, first_rows, second_rows, third_rows):
    khatri = (second_rows[:, None, :].astype(jnp.float32) * third_rows[None, :, :].astype(jnp.float32)).reshape(B * B, R).astype(jnp.bfloat16)
    product = jnp.dot(values, khatri, preferred_element_type=jnp.float32)
    return lax.optimization_barrier(jnp.sum(product.reshape(B, B, R) * first_rows[None, :, :].astype(jnp.float32), axis=1))

def reference(tensor_blocks, block_coords, live_count, owner_order, factor_two, factor_three, factor_four):
    devices = N_GRP * N_MEM
    table_two = factor_two.reshape(N_GRP, RBG, B, R)
    table_three = factor_three.reshape(N_GRP, RBG, B, R)
    table_four = factor_four.reshape(N_GRP, RBG, B, R)
    values_all = tensor_blocks.reshape(devices, NB, B * B, B * B)
    coords_all = block_coords.reshape(4, devices, NB)
    live_all = live_count.reshape(devices)
    slab_index = jnp.arange(SLAB, dtype=jnp.int32)

    def per_device(totals, device):
        group = device // N_MEM
        member = device % N_MEM
        owner_ids = lax.dynamic_index_in_dim(owner_order, member, 0, keepdims=False)

        def per_block(block, inner):
            slab_id = coords_all[0, device, block]
            position = jnp.sum(jnp.where(owner_ids == slab_id, slab_index, 0)).astype(jnp.int32)
            partial_value = block_partial(values_all[device, block], table_two[group, coords_all[1, device, block]], table_three[group, coords_all[2, device, block]], table_four[group, coords_all[3, device, block]])
            return inner.at[member, position].add(partial_value)
        return (lax.fori_loop(jnp.int32(0), live_all[device].astype(jnp.int32), per_block, totals), None)
    totals = jnp.zeros((N_MEM, SLAB, B, R), jnp.float32)
    totals = lax.scan(per_device, totals, jnp.arange(devices, dtype=jnp.int32))[0]
    system = gram_matrix(factor_two) * gram_matrix(factor_three) * gram_matrix(factor_four)
    solved = solve_rows(system, totals.reshape(N_MEM * SLAB * B, R))
    return solved.reshape(N_MEM, SLAB * B, R)
```

```python
import functools

import jax
import jax.numpy as jnp
from jax import lax
from jax.experimental import pallas as pl
from jax.experimental.pallas import tpu as pltpu
from jax.sharding import PartitionSpec as P

B = 16
R = 256
HALF = 128
OWNED = 4
NONE = 9999
MESH = pl.DeviceIdType.MESH


def dot_full(a, b, along_a=1, along_b=0):
    return lax.dot_general(
        a,
        b,
        (((along_a,), (along_b,)), ((), ())),
        precision=lax.Precision.HIGHEST,
        preferred_element_type=jnp.float32,
    )


def invert_half(ref):
    panels = HALF // 8
    lane = lax.broadcasted_iota(jnp.int32, (8, HALF), 1)
    row = lax.broadcasted_iota(jnp.int32, (8, HALF), 0)
    for panel in range(panels):
        first = panel * 8
        whole = ref[...]
        columns = [
            jnp.broadcast_to(whole[:, first + j : first + j + 1], (HALF, HALF)) for j in range(8)
        ]
        corner = [column[first : first + 8] for column in columns]
        inside = (lane >= first) & (lane < first + 8)
        pivots = jnp.where(
            inside, jnp.where(lane - first == row, 1.0, 0.0), whole[first : first + 8]
        )
        for j in range(8):
            inverse = 1.0 / jnp.broadcast_to(corner[j][j : j + 1], (8, HALF))
            scaled = jnp.broadcast_to(pivots[j : j + 1], (8, HALF)) * inverse
            here = row == j
            pivots = jnp.where(here, scaled, pivots - corner[j] * scaled)
            for k in range(j + 1, 8):
                factor = jnp.broadcast_to(corner[k][j : j + 1], (8, HALF)) * inverse
                corner[k] = jnp.where(here, factor, corner[k] - corner[j] * factor)
        for i in range(panels):
            at = i * 8
            if i == panel:
                ref[at : at + 8, :] = pivots
            else:
                part = jnp.where(inside, 0.0, whole[at : at + 8])
                for j in range(8):
                    part = part - columns[j][at : at + 8] * jnp.broadcast_to(
                        pivots[j : j + 1], (8, HALF)
                    )
                ref[at : at + 8, :] = part


def solve_kernel(system_ref, sums_ref, out_ref, first_ref, second_ref):
    first_ref[...] = system_ref[0:HALF, 0:HALF]
    invert_half(first_ref)
    first = first_ref[...]
    cross = system_ref[0:HALF, HALF:R]
    weights = dot_full(first, cross)
    second_ref[...] = system_ref[HALF:R, HALF:R] - dot_full(cross, weights, 0, 0)
    left = sums_ref[:, 0:HALF]
    invert_half(second_ref)
    right = dot_full(sums_ref[:, HALF:R] - dot_full(left, weights), second_ref[...])
    out_ref[:, HALF:R] = right
    out_ref[:, 0:HALF] = dot_full(left, first) - dot_full(right, weights, 1, 1)


def solve_rows(system, sums):
    return pl.pallas_call(
        solve_kernel,
        out_shape=jax.ShapeDtypeStruct(sums.shape, jnp.float32),
        scratch_shapes=[pltpu.VMEM((HALF, HALF), jnp.float32)] * 2,
        name="solve_rows",
    )(system, sums)


def gather_kernel(
    groups,
    members,
    coords_ref,
    live_ref,
    order_ref,
    blocks_ref,
    two_ref,
    three_ref,
    four_ref,
    system_ref,
    sums_ref,
    blocks,
    table,
    parts,
    gram_out,
    gram_in,
    system,
    rows_out,
    rows_in,
    code_out,
    code_in,
    lows,
    highs,
    block_sem,
    ring_send,
    ring_recv,
    gram_send,
    gram_recv,
    system_send,
    system_recv,
    rows_send,
    rows_recv,
    code_send,
    code_recv,
):
    group = lax.axis_index("grp")
    member = lax.axis_index("mem")
    slots = blocks.shape[0]
    owned = two_ref.shape[0] // B
    half_way = members // 2
    after = lax.rem(member + 1, members)
    before = lax.rem(member + members - 1, members)

    load = pltpu.make_async_copy(blocks_ref, blocks, block_sem)
    load.start()

    barrier = pltpu.get_barrier_semaphore()
    for neighbour in (after, before):
        pl.semaphore_signal(barrier, inc=1, device_id={"mem": neighbour}, device_id_type=MESH)

    def greet(step, carry):
        pl.semaphore_signal(
            barrier,
            inc=1,
            device_id={"grp": lax.rem(group + step, groups)},
            device_id_type=MESH,
        )
        return carry

    lax.fori_loop(1, groups, greet, 0)
    for mode, ref in enumerate((two_ref, three_ref, four_ref)):
        for i in range(owned):
            table[mode, member * owned + i] = ref[i * B : (i + 1) * B, :]
    pl.semaphore_wait(barrier, groups + 1)

    def hop(way, step, mode, source):
        chunk = table.at[mode, pl.ds(source * owned, owned)]
        return pltpu.make_async_remote_copy(
            src_ref=chunk,
            dst_ref=chunk,
            send_sem=ring_send.at[way, step, mode],
            recv_sem=ring_recv.at[way, step, mode],
            device_id={"mem": after if way == 0 else before},
            device_id_type=MESH,
        )

    def sent(way, step):
        shift = step if way == 1 else members - step
        return lax.rem(member + shift, members)

    def arrived(way, step):
        shift = step + 1 if way == 1 else members - step - 1
        return lax.rem(member + shift, members)

    def last_way(mode):
        return 0 if mode < 2 else 1

    for mode in range(3):
        for way in range(2):
            hop(way, 0, mode, sent(way, 0)).start()

    live = live_ref[0, 0]
    wanted = [coords_ref[0, j] for j in range(slots)]

    def find(place, found):
        here = order_ref[0, place]
        return tuple(jnp.where(here == c, place, f) for c, f in zip(wanted, found))

    found = lax.fori_loop(0, groups * OWNED, find, (jnp.int32(0),) * slots, unroll=4)
    places = [jnp.where(j < live, found[j], -NONE) for j in range(slots)]
    code_row = lax.broadcasted_iota(jnp.int32, (8, R), 0)

    def send_to(buffer_out, buffer_in, send_sem, recv_sem, target):
        return pltpu.make_async_remote_copy(
            src_ref=buffer_out.at[target],
            dst_ref=buffer_in.at[group],
            send_sem=send_sem.at[target],
            recv_sem=recv_sem.at[group],
            device_id={"grp": target},
            device_id_type=MESH,
        )

    def received(buffer_out, buffer_in, send_sem, recv_sem, source):
        return pltpu.make_async_remote_copy(
            src_ref=buffer_out.at[source],
            dst_ref=buffer_in.at[source],
            send_sem=send_sem.at[source],
            recv_sem=recv_sem.at[source],
            device_id={"grp": source},
            device_id_type=MESH,
        )

    gram_set = (gram_out, gram_in, gram_send, gram_recv)
    rows_set = (rows_out, rows_in, rows_send, rows_recv)
    code_set = (code_out, code_in, code_send, code_recv)

    def start_all(buffers):
        def one(step, carry):
            send_to(*buffers, lax.rem(group + step, groups)).start()
            return carry

        lax.fori_loop(1, groups, one, 0)

    def wait_all(buffers, way):
        def one(step, carry):
            copy = received(*buffers, lax.rem(group + step, groups))
            if way == "recv":
                copy.wait_recv()
            else:
                copy.wait_send()
            return carry

        lax.fori_loop(1, groups, one, 0)

    def encode(owner, carry):
        low, high = jnp.int32(NONE), jnp.int32(-1)
        for j in range(slots):
            offset = places[j] - owner * OWNED
            mine = (offset >= 0) & (offset < OWNED)
            low = jnp.minimum(low, jnp.where(mine, offset, NONE))
            high = jnp.maximum(high, jnp.where(mine, offset, -1))
        high = jnp.where(high > low, high, NONE)
        lows[owner] = low
        highs[owner] = high
        code_out[owner] = jnp.where(code_row == 0, low, high)
        return carry

    lax.fori_loop(0, groups, encode, 0)
    start_all(code_set)

    def ring_step(step, carry):
        for mode in range(3):
            for way in range(2):
                hop(way, step - 1, mode, arrived(way, step - 1)).wait_recv()
                hop(way, step, mode, sent(way, step)).start()
        return carry

    lax.fori_loop(1, half_way - 1, ring_step, 0)
    end = half_way - 1
    for mode in range(3):
        for way in range(2):
            hop(way, end - 1, mode, arrived(way, end - 1)).wait_recv()
            if way == last_way(mode):
                hop(way, end, mode, sent(way, end)).start()
    for mode in range(3):
        way = last_way(mode)
        hop(way, end, mode, arrived(way, end)).wait_recv()

    height = R // groups
    for mode in range(3):
        factor = table[mode].reshape(owned * members * B, R)
        gram = lax.dot_general(
            factor, factor, (((0,), (0,)), ((), ())), preferred_element_type=jnp.float32
        )
        gram_out[:, mode] = gram.reshape(groups, height, R)
    start_all(gram_set)
    load.wait()

    def one_slot(j, carry):
        third = table[1, coords_ref[2, j]].astype(jnp.float32)
        fourth = table[2, coords_ref[3, j]].astype(jnp.float32)
        khatri = (third[:, None, :] * fourth[None, :, :]).reshape(B * B, R).astype(jnp.bfloat16)
        product = jnp.dot(blocks[j], khatri, preferred_element_type=jnp.float32)
        second = table[0, coords_ref[1, j]].astype(jnp.float32)
        parts[j] = jnp.sum(product.reshape(B, B, R) * second[None, :, :], axis=1)
        return carry

    lax.fori_loop(0, slots, one_slot, 0)

    def pack(owner, carry):
        values = [parts[j] for j in range(slots)]
        for slot, chosen in enumerate((lows[owner], highs[owner])):
            total = jnp.zeros((B, R), jnp.float32)
            for j in range(slots):
                total = total + jnp.where(places[j] - owner * OWNED == chosen, values[j], 0.0)
            rows_out[owner, slot] = total.astype(jnp.bfloat16)
        return carry

    lax.fori_loop(0, groups, pack, 0)

    wait_all(gram_set, "recv")

    def add_gram(step, total):
        return total + gram_in[lax.rem(group + step, groups)]

    total = lax.fori_loop(1, groups, add_gram, gram_out[group])
    system[group] = total[0] * total[1] * total[2]

    def system_copy(index, target):
        return pltpu.make_async_remote_copy(
            src_ref=system.at[index],
            dst_ref=system.at[index],
            send_sem=system_send.at[target],
            recv_sem=system_recv.at[index],
            device_id={"grp": target},
            device_id_type=MESH,
        )

    def system_start(step, carry):
        system_copy(group, lax.rem(group + step, groups)).start()
        return carry

    lax.fori_loop(1, groups, system_start, 0)
    start_all(rows_set)

    def system_wait(step, carry):
        other = lax.rem(group + step, groups)
        system_copy(other, other).wait_recv()
        return carry

    lax.fori_loop(1, groups, system_wait, 0)
    system_ref[...] = system[...].reshape(R, R)

    wait_all(code_set, "recv")
    wait_all(rows_set, "recv")
    rows_in[group] = rows_out[group]
    code_in[group] = code_out[group]

    def add_rows(source, totals):
        code = code_in[source]
        for slot in range(2):
            values = rows_in[source, slot].astype(jnp.float32)
            place = jnp.broadcast_to(code[slot : slot + 1], (B, R))
            totals = tuple(
                t + jnp.where(place == p, values, 0.0) for p, t in enumerate(totals)
            )
        return totals

    totals = lax.fori_loop(0, groups, add_rows, (jnp.zeros((B, R), jnp.float32),) * OWNED)
    for p in range(OWNED):
        sums_ref[p * B : (p + 1) * B, :] = totals[p]

    wait_all(code_set, "send")
    wait_all(gram_set, "send")
    wait_all(rows_set, "send")

    def system_sent(step, carry):
        other = lax.rem(group + step, groups)
        system_copy(group, other).wait_send()
        return carry

    lax.fori_loop(1, groups, system_sent, 0)

    def ring_sent(step, carry):
        for mode in range(3):
            for way in range(2):
                hop(way, step, mode, sent(way, step)).wait_send()
        return carry

    lax.fori_loop(0, end, ring_sent, 0)
    for mode in range(3):
        way = last_way(mode)
        hop(way, end, mode, sent(way, end)).wait_send()


def on_device(
    tensor_blocks, block_coords, live_count, owner_order, factor_two, factor_three, factor_four
):
    groups = lax.axis_size("grp")
    members = lax.axis_size("mem")
    slots = tensor_blocks.shape[0]
    owned = factor_two.shape[0] // B
    height = R // groups
    smem = pl.BlockSpec(memory_space=pltpu.SMEM)
    vmem = pl.BlockSpec(memory_space=pltpu.VMEM)
    dma = pltpu.SemaphoreType.DMA
    system, sums = pl.pallas_call(
        functools.partial(gather_kernel, groups, members),
        out_shape=(
            jax.ShapeDtypeStruct((R, R), jnp.float32),
            jax.ShapeDtypeStruct((OWNED * B, R), jnp.float32),
        ),
        in_specs=[smem, smem, smem, pl.BlockSpec(memory_space=pl.ANY), vmem, vmem, vmem],
        out_specs=(vmem, vmem),
        scratch_shapes=[
            pltpu.VMEM(tensor_blocks.shape, jnp.bfloat16),
            pltpu.VMEM((3, members * owned, B, R), jnp.bfloat16),
            pltpu.VMEM((slots, B, R), jnp.float32),
            pltpu.VMEM((groups, 3, height, R), jnp.float32),
            pltpu.VMEM((groups, 3, height, R), jnp.float32),
            pltpu.VMEM((groups, height, R), jnp.float32),
            pltpu.VMEM((groups, 2, B, R), jnp.bfloat16),
            pltpu.VMEM((groups, 2, B, R), jnp.bfloat16),
            pltpu.VMEM((groups, 8, R), jnp.int32),
            pltpu.VMEM((groups, 8, R), jnp.int32),
            pltpu.SMEM((groups,), jnp.int32),
            pltpu.SMEM((groups,), jnp.int32),
            dma,
            dma((2, members // 2, 3)),
            dma((2, members // 2, 3)),
        ]
        + [dma((groups,))] * 8,
        compiler_params=pltpu.CompilerParams(
            collective_id=0, has_side_effects=True, vmem_limit_bytes=40 << 20
        ),
        name="gather_rows",
    )(
        block_coords,
        live_count,
        owner_order,
        tensor_blocks,
        factor_two,
        factor_three,
        factor_four,
    )
    return solve_rows(system, sums)[None]


def solution(mesh):
    return jax.shard_map(
        on_device,
        mesh=mesh,
        in_specs=(
            P(("grp", "mem"), None, None),
            P(None, ("grp", "mem")),
            P("grp", "mem"),
            P("mem", None),
            P(("grp", "mem"), None),
            P(("grp", "mem"), None),
            P(("grp", "mem"), None),
        ),
        out_specs=P("mem", "grp", None),
        check_vma=False,
    )
```

```python
import functools

import jax
import jax.numpy as jnp
from jax import lax
from jax.experimental import pallas as pl
from jax.experimental.pallas import tpu as pltpu
from jax.sharding import PartitionSpec as P

B = 16
R = 256
HALF = 128
OWNED = 4
NONE = 9999
MESH = pl.DeviceIdType.MESH


def dot_full(a, b, along_a=1, along_b=0):
    return lax.dot_general(
        a,
        b,
        (((along_a,), (along_b,)), ((), ())),
        precision=lax.Precision.HIGHEST,
        preferred_element_type=jnp.float32,
    )


def invert_half(ref):
    panels = HALF // 8
    lane = lax.broadcasted_iota(jnp.int32, (8, HALF), 1)
    row = lax.broadcasted_iota(jnp.int32, (8, HALF), 0)
    for panel in range(panels):
        first = panel * 8
        whole = ref[...]
        columns = [
            jnp.broadcast_to(whole[:, first + j : first + j + 1], (HALF, HALF)) for j in range(8)
        ]
        corner = [column[first : first + 8] for column in columns]
        inside = (lane >= first) & (lane < first + 8)
        pivots = jnp.where(
            inside, jnp.where(lane - first == row, 1.0, 0.0), whole[first : first + 8]
        )
        for j in range(8):
            inverse = 1.0 / jnp.broadcast_to(corner[j][j : j + 1], (8, HALF))
            scaled = jnp.broadcast_to(pivots[j : j + 1], (8, HALF)) * inverse
            here = row == j
            pivots = jnp.where(here, scaled, pivots - corner[j] * scaled)
            for k in range(j + 1, 8):
                factor = jnp.broadcast_to(corner[k][j : j + 1], (8, HALF)) * inverse
                corner[k] = jnp.where(here, factor, corner[k] - corner[j] * factor)
        for i in range(panels):
            at = i * 8
            if i == panel:
                ref[at : at + 8, :] = pivots
            else:
                part = jnp.where(inside, 0.0, whole[at : at + 8])
                for j in range(8):
                    part = part - columns[j][at : at + 8] * jnp.broadcast_to(
                        pivots[j : j + 1], (8, HALF)
                    )
                ref[at : at + 8, :] = part


def update_kernel(
    groups,
    members,
    coords_hbm,
    live_hbm,
    order_hbm,
    blocks_hbm,
    two_hbm,
    three_hbm,
    four_hbm,
    out_ref,
    coords_ref,
    live_ref,
    order_ref,
    blocks,
    table,
    parts,
    gram_out,
    gram_in,
    system,
    rows_out,
    rows_in,
    code_out,
    code_in,
    lows,
    highs,
    first_ref,
    second_ref,
    load_sem,
    ring_send,
    ring_recv,
    gram_send,
    gram_recv,
    system_send,
    system_recv,
    rows_send,
    rows_recv,
    code_send,
    code_recv,
):
    group = lax.axis_index("grp")
    member = lax.axis_index("mem")
    slots = blocks.shape[0]
    owned = two_hbm.shape[0]

    def beside(shift):
        return lax.rem(member + members + shift, members)


    factor_loads = [
        pltpu.make_async_copy(
            ref, table.at[mode, pl.ds(member * owned, owned)], load_sem.at[mode]
        )
        for mode, ref in enumerate((two_hbm, three_hbm, four_hbm))
    ]
    index_loads = [
        pltpu.make_async_copy(ref, to, load_sem.at[3 + i])
        for i, (ref, to) in enumerate(
            ((coords_hbm, coords_ref), (live_hbm, live_ref), (order_hbm, order_ref))
        )
    ]
    load = pltpu.make_async_copy(blocks_hbm, blocks, load_sem.at[6])
    for copy in factor_loads + index_loads + [load]:
        copy.start()

    barrier = pltpu.get_barrier_semaphore()
    for shift in (1, 2, -1, -2):
        pl.semaphore_signal(barrier, inc=1, device_id={"mem": beside(shift)}, device_id_type=MESH)

    def greet(step, carry):
        pl.semaphore_signal(
            barrier,
            inc=1,
            device_id={"grp": lax.rem(group + step, groups)},
            device_id_type=MESH,
        )
        return carry

    lax.fori_loop(1, groups, greet, 0)
    for copy in factor_loads:
        copy.wait()
    pl.semaphore_wait(barrier, groups + 3)

    reach = (members // 2, members // 2 - 1)
    sign = (1, -1)

    def travel(way, distance, step, mode):
        chunk = table.at[mode, pl.ds(beside(-sign[way] * distance) * owned, owned)]
        return pltpu.make_async_remote_copy(
            src_ref=chunk,
            dst_ref=chunk,
            send_sem=ring_send.at[way, distance + step - 1, mode],
            recv_sem=ring_recv.at[way, distance + step - 1, mode],
            device_id={"mem": beside(sign[way] * step)},
            device_id_type=MESH,
        )

    def arrival(way, distance, mode):
        chunk = table.at[mode, pl.ds(beside(-sign[way] * distance) * owned, owned)]
        return pltpu.make_async_remote_copy(
            src_ref=chunk,
            dst_ref=chunk,
            send_sem=ring_send.at[way, distance - 1, mode],
            recv_sem=ring_recv.at[way, distance - 1, mode],
            device_id={"mem": beside(-sign[way])},
            device_id_type=MESH,
        )

    def relay(distance):
        for mode in range(3):
            for way in range(2):
                if 0 < distance <= reach[way]:
                    arrival(way, distance, mode).wait_recv()
                if distance + 2 <= reach[way]:
                    travel(way, distance, 2, mode).start()
        for mode in range(3):
            for way in range(2):
                if distance + 1 <= reach[way]:
                    travel(way, distance, 1, mode).start()

    relay(0)
    for copy in index_loads:
        copy.wait()

    live = live_ref[0, 0]
    wanted = [coords_ref[0, j] for j in range(slots)]

    def find(place, found):
        here = order_ref[0, place]
        return tuple(jnp.where(here == c, place, f) for c, f in zip(wanted, found))

    found = lax.fori_loop(0, groups * OWNED, find, (jnp.int32(0),) * slots, unroll=4)
    places = [jnp.where(j < live, found[j], -NONE) for j in range(slots)]
    code_row = lax.broadcasted_iota(jnp.int32, (8, R), 0)

    def send_to(buffer_out, buffer_in, send_sem, recv_sem, target):
        return pltpu.make_async_remote_copy(
            src_ref=buffer_out.at[target],
            dst_ref=buffer_in.at[group],
            send_sem=send_sem.at[target],
            recv_sem=recv_sem.at[group],
            device_id={"grp": target},
            device_id_type=MESH,
        )

    def received(buffer_out, buffer_in, send_sem, recv_sem, source):
        return pltpu.make_async_remote_copy(
            src_ref=buffer_out.at[source],
            dst_ref=buffer_in.at[source],
            send_sem=send_sem.at[source],
            recv_sem=recv_sem.at[source],
            device_id={"grp": source},
            device_id_type=MESH,
        )

    gram_set = (gram_out, gram_in, gram_send, gram_recv)
    rows_set = (rows_out, rows_in, rows_send, rows_recv)
    code_set = (code_out, code_in, code_send, code_recv)

    def start_all(buffers):
        def one(step, carry):
            send_to(*buffers, lax.rem(group + step, groups)).start()
            return carry

        lax.fori_loop(1, groups, one, 0)

    def from_other(step):
        return lax.rem(group + groups - step, groups)

    def wait_sent(buffers):
        def one(step, carry):
            received(*buffers, lax.rem(group + step, groups)).wait_send()
            return carry

        lax.fori_loop(1, groups, one, 0)

    def encode(owner, carry):
        low, high = jnp.int32(NONE), jnp.int32(-1)
        for j in range(slots):
            offset = places[j] - owner * OWNED
            mine = (offset >= 0) & (offset < OWNED)
            low = jnp.minimum(low, jnp.where(mine, offset, NONE))
            high = jnp.maximum(high, jnp.where(mine, offset, -1))
        high = jnp.where(high > low, high, NONE)
        lows[owner] = low
        highs[owner] = high
        code_out[owner] = jnp.where(code_row == 0, low, high)
        return carry

    lax.fori_loop(0, groups, encode, 0)
    start_all(code_set)

    for distance in range(2, reach[0] + 1, 2):
        relay(distance)
    for distance in range(1, reach[0] + 1, 2):
        for mode in range(3):
            for way in range(2):
                if distance <= reach[way]:
                    arrival(way, distance, mode).wait_recv()

    height = R // groups
    for mode in range(3):
        factor = table[mode].reshape(owned * members * B, R)
        gram = lax.dot_general(
            factor, factor, (((0,), (0,)), ((), ())), preferred_element_type=jnp.float32
        )
        gram_out[:, mode] = gram.reshape(groups, height, R)
    start_all(gram_set)
    load.wait()

    def one_slot(j, carry):
        third = table[1, coords_ref[2, j]].astype(jnp.float32)
        fourth = table[2, coords_ref[3, j]].astype(jnp.float32)
        khatri = (third[:, None, :] * fourth[None, :, :]).reshape(B * B, R).astype(jnp.bfloat16)
        product = jnp.dot(blocks[j], khatri, preferred_element_type=jnp.float32)
        second = table[0, coords_ref[1, j]].astype(jnp.float32)
        parts[j] = jnp.sum(product.reshape(B, B, R) * second[None, :, :], axis=1)
        return carry

    lax.fori_loop(0, slots, one_slot, 0)

    def pack(owner, carry):
        values = [parts[j] for j in range(slots)]
        for slot, chosen in enumerate((lows[owner], highs[owner])):
            total = jnp.zeros((B, R), jnp.float32)
            for j in range(slots):
                total = total + jnp.where(places[j] - owner * OWNED == chosen, values[j], 0.0)
            rows_out[owner, slot] = total.astype(jnp.bfloat16)
        return carry

    lax.fori_loop(0, groups, pack, 0)

    def add_gram(step, total):
        source = from_other(step)
        received(*gram_set, source).wait_recv()
        return total + gram_in[source]

    total = lax.fori_loop(1, groups, add_gram, gram_out[group])
    system[group] = total[0] * total[1] * total[2]

    def system_copy(index, target):
        return pltpu.make_async_remote_copy(
            src_ref=system.at[index],
            dst_ref=system.at[index],
            send_sem=system_send.at[target],
            recv_sem=system_recv.at[index],
            device_id={"grp": target},
            device_id_type=MESH,
        )

    def system_start(step, carry):
        system_copy(group, lax.rem(group + step, groups)).start()
        return carry

    lax.fori_loop(1, groups, system_start, 0)
    start_all(rows_set)

    def system_wait(step, carry):
        other = from_other(step)
        system_copy(other, other).wait_recv()
        return carry

    lax.fori_loop(1, groups, system_wait, 0)
    first_ref[...] = system[0 : groups // 2].reshape(HALF, R)[:, 0:HALF]
    invert_half(first_ref)
    first = first_ref[...]
    cross = system[0 : groups // 2].reshape(HALF, R)[:, HALF:R]
    weights = dot_full(first, cross)
    second_ref[...] = system[groups // 2 :].reshape(HALF, R)[:, HALF:R] - dot_full(
        cross, weights, 0, 0
    )
    invert_half(second_ref)

    def add_code(code, rows, totals):
        for slot in range(2):
            values = rows[slot].astype(jnp.float32)
            place = jnp.broadcast_to(code[slot : slot + 1], (B, R))
            totals = tuple(
                t + jnp.where(place == p, values, 0.0) for p, t in enumerate(totals)
            )
        return totals

    def add_rows(step, totals):
        source = from_other(step)
        received(*code_set, source).wait_recv()
        received(*rows_set, source).wait_recv()
        return add_code(code_in[source], rows_in[source], totals)

    totals = (jnp.zeros((B, R), jnp.float32),) * OWNED
    totals = add_code(code_out[group], rows_out[group], totals)
    totals = lax.fori_loop(1, groups, add_rows, totals)
    sums = jnp.concatenate(totals, axis=0)
    left = sums[:, 0:HALF]
    right = dot_full(sums[:, HALF:R] - dot_full(left, weights), second_ref[...])
    out_ref[:, HALF:R] = right
    out_ref[:, 0:HALF] = dot_full(left, first) - dot_full(right, weights, 1, 1)

    wait_sent(code_set)
    wait_sent(gram_set)
    wait_sent(rows_set)

    def system_sent(step, carry):
        other = lax.rem(group + step, groups)
        system_copy(group, other).wait_send()
        return carry

    lax.fori_loop(1, groups, system_sent, 0)

    for distance in range(1, reach[0] + 1):
        for mode in range(3):
            for way in range(2):
                if distance <= reach[way]:
                    arrival(way, distance, mode).wait_send()


def on_device(
    tensor_blocks, block_coords, live_count, owner_order, factor_two, factor_three, factor_four
):
    groups = lax.axis_size("grp")
    members = lax.axis_size("mem")
    slots = tensor_blocks.shape[0]
    owned = factor_two.shape[0] // B
    height = R // groups
    hbm = pl.BlockSpec(memory_space=pl.ANY)
    vmem = pl.BlockSpec(memory_space=pltpu.VMEM)
    dma = pltpu.SemaphoreType.DMA
    factors = [f.reshape(owned, B, R) for f in (factor_two, factor_three, factor_four)]
    solved = pl.pallas_call(
        functools.partial(update_kernel, groups, members),
        out_shape=jax.ShapeDtypeStruct((OWNED * B, R), jnp.float32),
        in_specs=[hbm] * 7,
        out_specs=vmem,
        scratch_shapes=[
            pltpu.SMEM(block_coords.shape, jnp.int32),
            pltpu.SMEM(live_count.shape, jnp.int32),
            pltpu.SMEM(owner_order.shape, jnp.int32),
            pltpu.VMEM(tensor_blocks.shape, jnp.bfloat16),
            pltpu.VMEM((3, members * owned, B, R), jnp.bfloat16),
            pltpu.VMEM((slots, B, R), jnp.float32),
            pltpu.VMEM((groups, 3, height, R), jnp.float32),
            pltpu.VMEM((groups, 3, height, R), jnp.float32),
            pltpu.VMEM((groups, height, R), jnp.float32),
            pltpu.VMEM((groups, 2, B, R), jnp.bfloat16),
            pltpu.VMEM((groups, 2, B, R), jnp.bfloat16),
            pltpu.VMEM((groups, 8, R), jnp.int32),
            pltpu.VMEM((groups, 8, R), jnp.int32),
            pltpu.SMEM((groups,), jnp.int32),
            pltpu.SMEM((groups,), jnp.int32),
            pltpu.VMEM((HALF, HALF), jnp.float32),
            pltpu.VMEM((HALF, HALF), jnp.float32),
            dma((7,)),
            dma((2, members // 2, 3)),
            dma((2, members // 2, 3)),
        ]
        + [dma((groups,))] * 8,
        compiler_params=pltpu.CompilerParams(
            collective_id=0, has_side_effects=True, vmem_limit_bytes=60 << 20
        ),
        name="update_rows",
    )(block_coords, live_count, owner_order, tensor_blocks, *factors)
    return solved[None]


def solution(mesh):
    return jax.shard_map(
        on_device,
        mesh=mesh,
        in_specs=(
            P(("grp", "mem"), None, None),
            P(None, ("grp", "mem")),
            P("grp", "mem"),
            P("mem", None),
            P(("grp", "mem"), None),
            P(("grp", "mem"), None),
            P(("grp", "mem"), None),
        ),
        out_specs=P("mem", "grp", None),
        check_vma=False,
    )
```

```python
import functools

import jax
import jax.numpy as jnp
from jax import lax
from jax.experimental import pallas as pl
from jax.experimental.pallas import tpu as pltpu
from jax.sharding import PartitionSpec as P

B = 16
R = 256
HALF = 128
OWNED = 4
NONE = 9999
MESH = pl.DeviceIdType.MESH


def dot_full(a, b, along_a=1, along_b=0):
    return lax.dot_general(
        a,
        b,
        (((along_a,), (along_b,)), ((), ())),
        precision=lax.Precision.HIGHEST,
        preferred_element_type=jnp.float32,
    )


def invert_half(ref):
    panels = HALF // 8
    lane = lax.broadcasted_iota(jnp.int32, (8, HALF), 1)
    row = lax.broadcasted_iota(jnp.int32, (8, HALF), 0)
    for panel in range(panels):
        first = panel * 8
        whole = ref[...]
        columns = [
            jnp.broadcast_to(whole[:, first + j : first + j + 1], (HALF, HALF)) for j in range(8)
        ]
        corner = [column[first : first + 8] for column in columns]
        inside = (lane >= first) & (lane < first + 8)
        pivots = jnp.where(
            inside, jnp.where(lane - first == row, 1.0, 0.0), whole[first : first + 8]
        )
        for j in range(8):
            inverse = 1.0 / jnp.broadcast_to(corner[j][j : j + 1], (8, HALF))
            scaled = jnp.broadcast_to(pivots[j : j + 1], (8, HALF)) * inverse
            here = row == j
            pivots = jnp.where(here, scaled, pivots - corner[j] * scaled)
            for k in range(j + 1, 8):
                factor = jnp.broadcast_to(corner[k][j : j + 1], (8, HALF)) * inverse
                corner[k] = jnp.where(here, factor, corner[k] - corner[j] * factor)
        for i in range(panels):
            at = i * 8
            if i == panel:
                ref[at : at + 8, :] = pivots
            else:
                part = jnp.where(inside, 0.0, whole[at : at + 8])
                for j in range(8):
                    part = part - columns[j][at : at + 8] * jnp.broadcast_to(
                        pivots[j : j + 1], (8, HALF)
                    )
                ref[at : at + 8, :] = part


def update_kernel(
    groups,
    members,
    coords_hbm,
    live_hbm,
    order_hbm,
    blocks_hbm,
    two_hbm,
    three_hbm,
    four_hbm,
    out_ref,
    coords_ref,
    live_ref,
    order_ref,
    blocks,
    table,
    parts,
    gram_out,
    gram_in,
    system,
    rows_out,
    rows_in,
    code_out,
    code_in,
    lows,
    highs,
    first_ref,
    second_ref,
    load_sem,
    ring_send,
    ring_recv,
    gram_send,
    gram_recv,
    system_send,
    system_recv,
    rows_send,
    rows_recv,
    code_send,
    code_recv,
):
    group = lax.axis_index("grp")
    member = lax.axis_index("mem")
    slots = blocks.shape[0]
    owned = two_hbm.shape[0]

    def beside(shift):
        return lax.rem(member + members + shift, members)


    factor_loads = [
        pltpu.make_async_copy(
            ref, table.at[mode, pl.ds(member * owned, owned)], load_sem.at[mode]
        )
        for mode, ref in enumerate((two_hbm, three_hbm, four_hbm))
    ]
    index_loads = [
        pltpu.make_async_copy(ref, to, load_sem.at[3 + i])
        for i, (ref, to) in enumerate(
            ((coords_hbm, coords_ref), (live_hbm, live_ref), (order_hbm, order_ref))
        )
    ]
    load = pltpu.make_async_copy(blocks_hbm, blocks, load_sem.at[6])
    for copy in factor_loads + index_loads + [load]:
        copy.start()

    barrier = pltpu.get_barrier_semaphore()
    for shift in (1, 2, -1, -2):
        pl.semaphore_signal(barrier, inc=1, device_id={"mem": beside(shift)}, device_id_type=MESH)

    def greet(step, carry):
        pl.semaphore_signal(
            barrier,
            inc=1,
            device_id={"grp": lax.rem(group + step, groups)},
            device_id_type=MESH,
        )
        return carry

    lax.fori_loop(1, groups, greet, 0, unroll=True)
    for copy in factor_loads:
        copy.wait()
    pl.semaphore_wait(barrier, groups + 3)

    reach = (members // 2, members // 2 - 1)
    sign = (1, -1)

    def travel(way, distance, step, mode):
        chunk = table.at[mode, pl.ds(beside(-sign[way] * distance) * owned, owned)]
        return pltpu.make_async_remote_copy(
            src_ref=chunk,
            dst_ref=chunk,
            send_sem=ring_send,
            recv_sem=ring_recv.at[way, distance + step - 1, mode],
            device_id={"mem": beside(sign[way] * step)},
            device_id_type=MESH,
        )

    def arrival(way, distance, mode):
        chunk = table.at[mode, pl.ds(beside(-sign[way] * distance) * owned, owned)]
        return pltpu.make_async_remote_copy(
            src_ref=chunk,
            dst_ref=chunk,
            send_sem=ring_send,
            recv_sem=ring_recv.at[way, distance - 1, mode],
            device_id={"mem": beside(-sign[way])},
            device_id_type=MESH,
        )

    def relay(distance):
        for mode in range(3):
            for way in range(2):
                if 0 < distance <= reach[way]:
                    arrival(way, distance, mode).wait_recv()
                if distance + 2 <= reach[way]:
                    travel(way, distance, 2, mode).start()
        for mode in range(3):
            for way in range(2):
                if distance + 1 <= reach[way]:
                    travel(way, distance, 1, mode).start()

    relay(0)
    for copy in index_loads:
        copy.wait()

    live = live_ref[0, 0]
    wanted = [coords_ref[0, j] for j in range(slots)]

    def find(place, found):
        here = order_ref[0, place]
        return tuple(jnp.where(here == c, place, f) for c, f in zip(wanted, found))

    found = lax.fori_loop(0, groups * OWNED, find, (jnp.int32(0),) * slots, unroll=4)
    places = [jnp.where(j < live, found[j], -NONE) for j in range(slots)]
    code_row = lax.broadcasted_iota(jnp.int32, (8, HALF), 0)

    def send_to(buffer_out, buffer_in, send_sem, recv_sem, target):
        return pltpu.make_async_remote_copy(
            src_ref=buffer_out.at[target],
            dst_ref=buffer_in.at[group],
            send_sem=send_sem,
            recv_sem=recv_sem,
            device_id={"grp": target},
            device_id_type=MESH,
        )

    def wait_others(buffer, sem):
        others = buffer.at[pl.ds(0, groups - 1)]
        pltpu.make_async_copy(others, others, sem).wait()

    gram_set = (gram_out, gram_in, gram_send, gram_recv)
    rows_set = (rows_out, rows_in, rows_send, rows_recv)
    code_set = (code_out, code_in, code_send, code_recv)

    def start_all(buffers):
        def one(step, carry):
            send_to(*buffers, lax.rem(group + step, groups)).start()
            return carry

        lax.fori_loop(1, groups, one, 0, unroll=True)

    def from_other(step):
        return lax.rem(group + groups - step, groups)

    def encode(owner, carry):
        low, high = jnp.int32(NONE), jnp.int32(-1)
        for j in range(slots):
            offset = places[j] - owner * OWNED
            mine = (offset >= 0) & (offset < OWNED)
            low = jnp.minimum(low, jnp.where(mine, offset, NONE))
            high = jnp.maximum(high, jnp.where(mine, offset, -1))
        high = jnp.where(high > low, high, NONE)
        lows[owner] = low
        highs[owner] = high
        code_out[owner] = jnp.where(code_row == 0, low, high)
        return carry

    lax.fori_loop(0, groups, encode, 0)
    start_all(code_set)

    for distance in range(2, reach[0], 2):
        relay(distance)
    height = R // groups
    for mode in range(3):
        for distance in range(1, reach[0] + 1, 2):
            for way in range(2):
                if distance <= reach[way]:
                    arrival(way, distance, mode).wait_recv()
        if reach[0] % 2 == 0:
            arrival(0, reach[0], mode).wait_recv()
        factor = table[mode].reshape(owned * members * B, R)
        gram = lax.dot_general(
            factor, factor, (((0,), (0,)), ((), ())), preferred_element_type=jnp.float32
        )
        gram_out[:, mode] = gram.reshape(groups, height, R)
    start_all(gram_set)
    load.wait()

    def one_slot(j, carry):
        third = table[1, coords_ref[2, j]].astype(jnp.float32)
        fourth = table[2, coords_ref[3, j]].astype(jnp.float32)
        khatri = (third[:, None, :] * fourth[None, :, :]).reshape(B * B, R).astype(jnp.bfloat16)
        product = jnp.dot(blocks[j], khatri, preferred_element_type=jnp.float32)
        second = table[0, coords_ref[1, j]].astype(jnp.float32)
        parts[j] = jnp.sum(product.reshape(B, B, R) * second[None, :, :], axis=1)
        return carry

    lax.fori_loop(0, slots, one_slot, 0)

    def pack(owner, carry):
        values = [parts[j] for j in range(slots)]
        for slot, chosen in enumerate((lows[owner], highs[owner])):
            total = jnp.zeros((B, R), jnp.float32)
            for j in range(slots):
                total = total + jnp.where(places[j] - owner * OWNED == chosen, values[j], 0.0)
            rows_out[owner, slot] = total.astype(jnp.bfloat16)
        return carry

    lax.fori_loop(0, groups, pack, 0)

    wait_others(gram_in, gram_recv)

    def add_gram(step, total):
        return total + gram_in[from_other(step)]

    total = lax.fori_loop(1, groups, add_gram, gram_out[group], unroll=True)
    system[group] = total[0] * total[1] * total[2]

    def system_copy(index, target):
        return pltpu.make_async_remote_copy(
            src_ref=system.at[index],
            dst_ref=system.at[index],
            send_sem=system_send,
            recv_sem=system_recv,
            device_id={"grp": target},
            device_id_type=MESH,
        )

    def system_start(step, carry):
        system_copy(group, lax.rem(group + step, groups)).start()
        return carry

    lax.fori_loop(1, groups, system_start, 0, unroll=True)
    start_all(rows_set)

    passed = table.at[:, pl.ds(0, (reach[0] + reach[1]) * owned)]
    pltpu.make_async_copy(passed, passed, ring_send).wait()
    wait_others(gram_out, gram_send)
    wait_others(code_out, code_send)
    wait_others(system, system_recv)
    first_ref[...] = system[0 : groups // 2].reshape(HALF, R)[:, 0:HALF]
    invert_half(first_ref)
    first = first_ref[...]
    cross = system[0 : groups // 2].reshape(HALF, R)[:, HALF:R]
    weights = dot_full(first, cross)
    second_ref[...] = system[groups // 2 :].reshape(HALF, R)[:, HALF:R] - dot_full(
        cross, weights, 0, 0
    )
    def add_code(code, rows, totals):
        for slot in range(2):
            values = rows[slot].astype(jnp.float32)
            place = jnp.broadcast_to(code[slot : slot + 1], (B, HALF))
            place = jnp.concatenate([place, place], axis=1)
            totals = tuple(
                t + jnp.where(place == p, values, 0.0) for p, t in enumerate(totals)
            )
        return totals

    def add_rows(step, totals):
        source = from_other(step)
        return add_code(code_in[source], rows_in[source], totals)

    totals = (jnp.zeros((B, R), jnp.float32),) * OWNED
    totals = add_code(code_out[group], rows_out[group], totals)
    wait_others(code_in, code_recv)
    wait_others(rows_in, rows_recv)
    wait_others(system, system_send)
    wait_others(rows_out, rows_send)
    totals = lax.fori_loop(1, groups, add_rows, totals, unroll=4)
    sums = jnp.concatenate(totals, axis=0)
    left = sums[:, 0:HALF]
    right = sums[:, HALF:R] - dot_full(left, weights)
    left = dot_full(left, first)
    invert_half(second_ref)
    right = dot_full(right, second_ref[...])

    out_ref[:, HALF:R] = right
    out_ref[:, 0:HALF] = left - dot_full(right, weights, 1, 1)


def on_device(
    tensor_blocks, block_coords, live_count, owner_order, factor_two, factor_three, factor_four
):
    groups = lax.axis_size("grp")
    members = lax.axis_size("mem")
    slots = tensor_blocks.shape[0]
    owned = factor_two.shape[0] // B
    height = R // groups
    hbm = pl.BlockSpec(memory_space=pl.ANY)
    vmem = pl.BlockSpec(memory_space=pltpu.VMEM)
    dma = pltpu.SemaphoreType.DMA
    factors = [f.reshape(owned, B, R) for f in (factor_two, factor_three, factor_four)]
    solved = pl.pallas_call(
        functools.partial(update_kernel, groups, members),
        out_shape=jax.ShapeDtypeStruct((OWNED * B, R), jnp.float32),
        in_specs=[hbm] * 7,
        out_specs=vmem,
        scratch_shapes=[
            pltpu.SMEM(block_coords.shape, jnp.int32),
            pltpu.SMEM(live_count.shape, jnp.int32),
            pltpu.SMEM(owner_order.shape, jnp.int32),
            pltpu.VMEM(tensor_blocks.shape, jnp.bfloat16),
            pltpu.VMEM((3, members * owned, B, R), jnp.bfloat16),
            pltpu.VMEM((slots, B, R), jnp.float32),
            pltpu.VMEM((groups, 3, height, R), jnp.float32),
            pltpu.VMEM((groups, 3, height, R), jnp.float32),
            pltpu.VMEM((groups, height, R), jnp.float32),
            pltpu.VMEM((groups, 2, B, R), jnp.bfloat16),
            pltpu.VMEM((groups, 2, B, R), jnp.bfloat16),
            pltpu.VMEM((groups, 8, HALF), jnp.int32),
            pltpu.VMEM((groups, 8, HALF), jnp.int32),
            pltpu.SMEM((groups,), jnp.int32),
            pltpu.SMEM((groups,), jnp.int32),
            pltpu.VMEM((HALF, HALF), jnp.float32),
            pltpu.VMEM((HALF, HALF), jnp.float32),
            dma((7,)),
            dma,
            dma((2, members // 2, 3)),
        ]
        + [dma] * 8,
        compiler_params=pltpu.CompilerParams(
            collective_id=0, has_side_effects=True, vmem_limit_bytes=60 << 20
        ),
        name="update_rows",
    )(block_coords, live_count, owner_order, tensor_blocks, *factors)
    return solved[None]


def solution(mesh):
    return jax.shard_map(
        on_device,
        mesh=mesh,
        in_specs=(
            P(("grp", "mem"), None, None),
            P(None, ("grp", "mem")),
            P("grp", "mem"),
            P("mem", None),
            P(("grp", "mem"), None),
            P(("grp", "mem"), None),
            P(("grp", "mem"), None),
        ),
        out_specs=P("mem", "grp", None),
        check_vma=False,
    )
```

```python
import functools

import jax
import jax.numpy as jnp
from jax import lax
from jax.experimental import pallas as pl
from jax.experimental.pallas import tpu as pltpu
from jax.sharding import PartitionSpec as P

B = 16
R = 256
HALF = 128
OWNED = 4
NONE = 9999
MESH = pl.DeviceIdType.MESH


def dot_full(a, b, along_a=1, along_b=0):
    return lax.dot_general(
        a,
        b,
        (((along_a,), (along_b,)), ((), ())),
        precision=lax.Precision.HIGHEST,
        preferred_element_type=jnp.float32,
    )


def invert_half(ref):
    panels = HALF // 8
    lane = lax.broadcasted_iota(jnp.int32, (8, HALF), 1)
    row = lax.broadcasted_iota(jnp.int32, (8, HALF), 0)
    for panel in range(panels):
        first = panel * 8
        whole = ref[...]
        columns = [
            jnp.broadcast_to(whole[:, first + j : first + j + 1], (HALF, HALF)) for j in range(8)
        ]
        corner = [column[first : first + 8] for column in columns]
        inside = (lane >= first) & (lane < first + 8)
        pivots = jnp.where(
            inside, jnp.where(lane - first == row, 1.0, 0.0), whole[first : first + 8]
        )
        for j in range(8):
            inverse = 1.0 / jnp.broadcast_to(corner[j][j : j + 1], (8, HALF))
            scaled = jnp.broadcast_to(pivots[j : j + 1], (8, HALF)) * inverse
            here = row == j
            pivots = jnp.where(here, scaled, pivots - corner[j] * scaled)
            for k in range(j + 1, 8):
                factor = jnp.broadcast_to(corner[k][j : j + 1], (8, HALF)) * inverse
                corner[k] = jnp.where(here, factor, corner[k] - corner[j] * factor)
        for i in range(panels):
            at = i * 8
            if i == panel:
                ref[at : at + 8, :] = pivots
            else:
                part = jnp.where(inside, 0.0, whole[at : at + 8])
                for j in range(8):
                    part = part - columns[j][at : at + 8] * jnp.broadcast_to(
                        pivots[j : j + 1], (8, HALF)
                    )
                ref[at : at + 8, :] = part


def update_kernel(
    groups,
    members,
    coords_hbm,
    live_hbm,
    order_hbm,
    blocks_hbm,
    two_hbm,
    three_hbm,
    four_hbm,
    out_ref,
    coords_ref,
    live_ref,
    order_ref,
    blocks,
    table,
    parts,
    gram_out,
    gram_in,
    system,
    rows_out,
    rows_in,
    code_out,
    code_in,
    lows,
    highs,
    first_ref,
    second_ref,
    load_sem,
    ring_send,
    ring_recv,
    gram_send,
    gram_recv,
    system_send,
    system_recv,
    rows_send,
    rows_recv,
    code_send,
    code_recv,
):
    group = lax.axis_index("grp")
    member = lax.axis_index("mem")
    slots = blocks.shape[0]
    owned = two_hbm.shape[0]

    def beside(shift):
        return lax.rem(member + members + shift, members)


    factor_loads = [
        pltpu.make_async_copy(
            ref, table.at[mode, pl.ds(member * owned, owned)], load_sem.at[mode]
        )
        for mode, ref in enumerate((two_hbm, three_hbm, four_hbm))
    ]
    index_loads = [
        pltpu.make_async_copy(ref, to, load_sem.at[3 + i])
        for i, (ref, to) in enumerate(
            ((coords_hbm, coords_ref), (live_hbm, live_ref), (order_hbm, order_ref))
        )
    ]
    load = pltpu.make_async_copy(blocks_hbm, blocks, load_sem.at[6])
    for copy in factor_loads + index_loads + [load]:
        copy.start()

    barrier = pltpu.get_barrier_semaphore()
    for shift in (1, 2, -1, -2):
        pl.semaphore_signal(barrier, inc=1, device_id={"mem": beside(shift)}, device_id_type=MESH)

    def greet(step, carry):
        pl.semaphore_signal(
            barrier,
            inc=1,
            device_id={"grp": lax.rem(group + step, groups)},
            device_id_type=MESH,
        )
        return carry

    lax.fori_loop(1, groups, greet, 0, unroll=True)
    for copy in factor_loads:
        copy.wait()
    pl.semaphore_wait(barrier, groups + 3)

    reach = (members // 2, members // 2 - 1)
    sign = (1, -1)

    def travel(way, distance, step, mode):
        chunk = table.at[mode, pl.ds(beside(-sign[way] * distance) * owned, owned)]
        return pltpu.make_async_remote_copy(
            src_ref=chunk,
            dst_ref=chunk,
            send_sem=ring_send,
            recv_sem=ring_recv.at[way, distance + step - 1, mode],
            device_id={"mem": beside(sign[way] * step)},
            device_id_type=MESH,
        )

    def arrival(way, distance, mode):
        chunk = table.at[mode, pl.ds(beside(-sign[way] * distance) * owned, owned)]
        return pltpu.make_async_remote_copy(
            src_ref=chunk,
            dst_ref=chunk,
            send_sem=ring_send,
            recv_sem=ring_recv.at[way, distance - 1, mode],
            device_id={"mem": beside(-sign[way])},
            device_id_type=MESH,
        )

    def relay(distance):
        for mode in range(3):
            for way in range(2):
                if 0 < distance <= reach[way]:
                    arrival(way, distance, mode).wait_recv()
                if distance + 2 <= reach[way]:
                    travel(way, distance, 2, mode).start()
        for mode in range(3):
            for way in range(2):
                if distance + 1 <= reach[way]:
                    travel(way, distance, 1, mode).start()

    relay(0)
    for copy in index_loads:
        copy.wait()

    live = live_ref[0, 0]
    wanted = [coords_ref[0, j] for j in range(slots)]

    def find(place, found):
        here = order_ref[0, place]
        return tuple(jnp.where(here == c, place, f) for c, f in zip(wanted, found))

    found = lax.fori_loop(0, groups * OWNED, find, (jnp.int32(0),) * slots, unroll=4)
    places = [jnp.where(j < live, found[j], -NONE) for j in range(slots)]
    code_row = lax.broadcasted_iota(jnp.int32, (8, HALF), 0)

    def send_to(buffer_out, buffer_in, send_sem, recv_sem, target):
        return pltpu.make_async_remote_copy(
            src_ref=buffer_out.at[target],
            dst_ref=buffer_in.at[group],
            send_sem=send_sem,
            recv_sem=recv_sem,
            device_id={"grp": target},
            device_id_type=MESH,
        )

    def wait_others(buffer, sem):
        others = buffer.at[pl.ds(0, groups - 1)]
        pltpu.make_async_copy(others, others, sem).wait()

    rows_set = (rows_out, rows_in, rows_send, rows_recv)
    code_set = (code_out, code_in, code_send, code_recv)

    def start_all(buffers):
        def one(step, carry):
            send_to(*buffers, lax.rem(group + step, groups)).start()
            return carry

        lax.fori_loop(1, groups, one, 0, unroll=True)

    def from_other(step):
        return lax.rem(group + groups - step, groups)

    def encode(owner, carry):
        low, high = jnp.int32(NONE), jnp.int32(-1)
        for j in range(slots):
            offset = places[j] - owner * OWNED
            mine = (offset >= 0) & (offset < OWNED)
            low = jnp.minimum(low, jnp.where(mine, offset, NONE))
            high = jnp.maximum(high, jnp.where(mine, offset, -1))
        high = jnp.where(high > low, high, NONE)
        lows[owner] = low
        highs[owner] = high
        code_out[owner] = jnp.where(code_row == 0, low, high)
        return carry

    lax.fori_loop(0, groups, encode, 0)
    start_all(code_set)

    for distance in range(2, reach[0], 2):
        relay(distance)
    gram_parts = {0: (0, 1), 2: (1, 2)}

    def start_gram(start, count):
        def one(step, carry):
            target = lax.rem(group + step, groups)
            pltpu.make_async_remote_copy(
                src_ref=gram_out.at[target, pl.ds(start, count)],
                dst_ref=gram_in.at[group, pl.ds(start, count)],
                send_sem=gram_send,
                recv_sem=gram_recv,
                device_id={"grp": target},
                device_id_type=MESH,
            ).start()
            return carry

        lax.fori_loop(1, groups, one, 0, unroll=True)

    height = R // groups
    for mode in range(3):
        for distance in range(1, reach[0] + 1, 2):
            for way in range(2):
                if distance <= reach[way]:
                    arrival(way, distance, mode).wait_recv()
        if reach[0] % 2 == 0:
            arrival(0, reach[0], mode).wait_recv()
        factor = table[mode].reshape(owned * members * B, R)
        gram = lax.dot_general(
            factor, factor, (((0,), (0,)), ((), ())), preferred_element_type=jnp.float32
        )
        gram_out[:, mode] = gram.reshape(groups, height, R)
        if mode in gram_parts:
            start_gram(*gram_parts[mode])
    load.wait()

    def one_slot(j, carry):
        third = table[1, coords_ref[2, j]].astype(jnp.float32)
        fourth = table[2, coords_ref[3, j]].astype(jnp.float32)
        khatri = (third[:, None, :] * fourth[None, :, :]).reshape(B * B, R).astype(jnp.bfloat16)
        product = jnp.dot(blocks[j], khatri, preferred_element_type=jnp.float32)
        second = table[0, coords_ref[1, j]].astype(jnp.float32)
        parts[j] = jnp.sum(product.reshape(B, B, R) * second[None, :, :], axis=1)
        return carry

    lax.fori_loop(0, slots, one_slot, 0)

    def pack(owner, carry):
        values = [parts[j] for j in range(slots)]
        for slot, chosen in enumerate((lows[owner], highs[owner])):
            total = jnp.zeros((B, R), jnp.float32)
            for j in range(slots):
                total = total + jnp.where(places[j] - owner * OWNED == chosen, values[j], 0.0)
            rows_out[owner, slot] = total.astype(jnp.bfloat16)
        return carry

    lax.fori_loop(0, groups, pack, 0)

    wait_others(gram_in, gram_recv)

    def add_gram(step, total):
        return total + gram_in[from_other(step)]

    total = lax.fori_loop(1, groups, add_gram, gram_out[group], unroll=True)
    system[group] = total[0] * total[1] * total[2]

    def system_copy(index, target):
        return pltpu.make_async_remote_copy(
            src_ref=system.at[index],
            dst_ref=system.at[index],
            send_sem=system_send,
            recv_sem=system_recv,
            device_id={"grp": target},
            device_id_type=MESH,
        )

    def system_start(step, carry):
        system_copy(group, lax.rem(group + step, groups)).start()
        return carry

    lax.fori_loop(1, groups, system_start, 0, unroll=True)
    start_all(rows_set)

    passed = table.at[:, pl.ds(0, (reach[0] + reach[1]) * owned)]
    pltpu.make_async_copy(passed, passed, ring_send).wait()
    wait_others(gram_out, gram_send)
    wait_others(code_out, code_send)
    wait_others(system, system_recv)
    first_ref[...] = system[0 : groups // 2].reshape(HALF, R)[:, 0:HALF]
    invert_half(first_ref)
    first = first_ref[...]
    cross = system[0 : groups // 2].reshape(HALF, R)[:, HALF:R]
    weights = dot_full(first, cross)
    second_ref[...] = system[groups // 2 :].reshape(HALF, R)[:, HALF:R] - dot_full(
        cross, weights, 0, 0
    )
    def add_code(code, rows, totals):
        for slot in range(2):
            values = rows[slot].astype(jnp.float32)
            place = jnp.broadcast_to(code[slot : slot + 1], (B, HALF))
            place = jnp.concatenate([place, place], axis=1)
            totals = tuple(
                t + jnp.where(place == p, values, 0.0) for p, t in enumerate(totals)
            )
        return totals

    def add_rows(step, totals):
        source = from_other(step)
        return add_code(code_in[source], rows_in[source], totals)

    totals = (jnp.zeros((B, R), jnp.float32),) * OWNED
    totals = add_code(code_out[group], rows_out[group], totals)
    wait_others(code_in, code_recv)
    wait_others(rows_in, rows_recv)
    wait_others(system, system_send)
    wait_others(rows_out, rows_send)
    totals = lax.fori_loop(1, groups, add_rows, totals, unroll=4)
    sums = jnp.concatenate(totals, axis=0)
    left = sums[:, 0:HALF]
    right = sums[:, HALF:R] - dot_full(left, weights)
    left = dot_full(left, first)
    invert_half(second_ref)
    right = dot_full(right, second_ref[...])

    out_ref[:, HALF:R] = right
    out_ref[:, 0:HALF] = left - dot_full(right, weights, 1, 1)


def on_device(
    tensor_blocks, block_coords, live_count, owner_order, factor_two, factor_three, factor_four
):
    groups = lax.axis_size("grp")
    members = lax.axis_size("mem")
    slots = tensor_blocks.shape[0]
    owned = factor_two.shape[0] // B
    height = R // groups
    hbm = pl.BlockSpec(memory_space=pl.ANY)
    vmem = pl.BlockSpec(memory_space=pltpu.VMEM)
    dma = pltpu.SemaphoreType.DMA
    factors = [f.reshape(owned, B, R) for f in (factor_two, factor_three, factor_four)]
    solved = pl.pallas_call(
        functools.partial(update_kernel, groups, members),
        out_shape=jax.ShapeDtypeStruct((OWNED * B, R), jnp.float32),
        in_specs=[hbm] * 7,
        out_specs=vmem,
        scratch_shapes=[
            pltpu.SMEM(block_coords.shape, jnp.int32),
            pltpu.SMEM(live_count.shape, jnp.int32),
            pltpu.SMEM(owner_order.shape, jnp.int32),
            pltpu.VMEM(tensor_blocks.shape, jnp.bfloat16),
            pltpu.VMEM((3, members * owned, B, R), jnp.bfloat16),
            pltpu.VMEM((slots, B, R), jnp.float32),
            pltpu.VMEM((groups, 3, height, R), jnp.float32),
            pltpu.VMEM((groups, 3, height, R), jnp.float32),
            pltpu.VMEM((groups, height, R), jnp.float32),
            pltpu.VMEM((groups, 2, B, R), jnp.bfloat16),
            pltpu.VMEM((groups, 2, B, R), jnp.bfloat16),
            pltpu.VMEM((groups, 8, HALF), jnp.int32),
            pltpu.VMEM((groups, 8, HALF), jnp.int32),
            pltpu.SMEM((groups,), jnp.int32),
            pltpu.SMEM((groups,), jnp.int32),
            pltpu.VMEM((HALF, HALF), jnp.float32),
            pltpu.VMEM((HALF, HALF), jnp.float32),
            dma((7,)),
            dma,
            dma((2, members // 2, 3)),
        ]
        + [dma] * 8,
        compiler_params=pltpu.CompilerParams(
            collective_id=0, has_side_effects=True, vmem_limit_bytes=60 << 20
        ),
        name="update_rows",
    )(block_coords, live_count, owner_order, tensor_blocks, *factors)
    return solved[None]


def solution(mesh):
    return jax.shard_map(
        on_device,
        mesh=mesh,
        in_specs=(
            P(("grp", "mem"), None, None),
            P(None, ("grp", "mem")),
            P("grp", "mem"),
            P("mem", None),
            P(("grp", "mem"), None),
            P(("grp", "mem"), None),
            P(("grp", "mem"), None),
        ),
        out_specs=P("mem", "grp", None),
        check_vma=False,
    )
```

```python
import functools

import jax
import jax.numpy as jnp
from jax import lax
from jax.experimental import pallas as pl
from jax.experimental.pallas import tpu as pltpu
from jax.sharding import PartitionSpec as P

B = 16
R = 256
HALF = 128
OWNED = 4
NONE = 9999
MESH = pl.DeviceIdType.MESH


def dot_full(a, b, along_a=1, along_b=0):
    return lax.dot_general(
        a,
        b,
        (((along_a,), (along_b,)), ((), ())),
        precision=lax.Precision.HIGHEST,
        preferred_element_type=jnp.float32,
    )


def invert_half(ref):
    panels = HALF // 8
    lane = lax.broadcasted_iota(jnp.int32, (8, HALF), 1)
    row = lax.broadcasted_iota(jnp.int32, (8, HALF), 0)
    for panel in range(panels):
        first = panel * 8
        whole = ref[...]
        columns = [
            jnp.broadcast_to(whole[:, first + j : first + j + 1], (HALF, HALF)) for j in range(8)
        ]
        corner = [column[first : first + 8] for column in columns]
        inside = (lane >= first) & (lane < first + 8)
        pivots = jnp.where(
            inside, jnp.where(lane - first == row, 1.0, 0.0), whole[first : first + 8]
        )
        for j in range(8):
            inverse = 1.0 / jnp.broadcast_to(corner[j][j : j + 1], (8, HALF))
            scaled = jnp.broadcast_to(pivots[j : j + 1], (8, HALF)) * inverse
            here = row == j
            pivots = jnp.where(here, scaled, pivots - corner[j] * scaled)
            for k in range(j + 1, 8):
                factor = jnp.broadcast_to(corner[k][j : j + 1], (8, HALF)) * inverse
                corner[k] = jnp.where(here, factor, corner[k] - corner[j] * factor)
        for i in range(panels):
            at = i * 8
            if i == panel:
                ref[at : at + 8, :] = pivots
            else:
                part = jnp.where(inside, 0.0, whole[at : at + 8])
                for j in range(8):
                    part = part - columns[j][at : at + 8] * jnp.broadcast_to(
                        pivots[j : j + 1], (8, HALF)
                    )
                ref[at : at + 8, :] = part


def update_kernel(
    groups,
    members,
    coords_hbm,
    live_hbm,
    order_hbm,
    blocks_hbm,
    two_hbm,
    three_hbm,
    four_hbm,
    out_ref,
    coords_ref,
    live_ref,
    order_ref,
    blocks,
    table,
    parts,
    gram_out,
    gram_in,
    system,
    rows_out,
    rows_in,
    code_out,
    code_in,
    lows,
    highs,
    first_ref,
    second_ref,
    load_sem,
    ring_send,
    ring_recv,
    gram_send,
    gram_recv,
    system_send,
    system_recv,
    rows_send,
    rows_recv,
    code_send,
    code_recv,
):
    group = lax.axis_index("grp")
    member = lax.axis_index("mem")
    slots = blocks.shape[0]
    owned = two_hbm.shape[0]

    def beside(shift):
        return lax.rem(member + members + shift, members)


    factor_loads = [
        pltpu.make_async_copy(
            ref, table.at[mode, pl.ds(member * owned, owned)], load_sem.at[mode]
        )
        for mode, ref in enumerate((two_hbm, three_hbm, four_hbm))
    ]
    index_loads = [
        pltpu.make_async_copy(ref, to, load_sem.at[3 + i])
        for i, (ref, to) in enumerate(
            ((coords_hbm, coords_ref), (live_hbm, live_ref), (order_hbm, order_ref))
        )
    ]
    load = pltpu.make_async_copy(blocks_hbm, blocks, load_sem.at[6])
    for copy in factor_loads + index_loads + [load]:
        copy.start()

    barrier = pltpu.get_barrier_semaphore()
    for shift in (1, 2, -1, -2):
        pl.semaphore_signal(barrier, inc=1, device_id={"mem": beside(shift)}, device_id_type=MESH)

    def greet(step, carry):
        pl.semaphore_signal(
            barrier,
            inc=1,
            device_id={"grp": lax.rem(group + step, groups)},
            device_id_type=MESH,
        )
        return carry

    lax.fori_loop(1, groups, greet, 0, unroll=True)
    for copy in factor_loads:
        copy.wait()
    pl.semaphore_wait(barrier, groups + 3)

    reach = (members // 2, members // 2 - 1)
    sign = (1, -1)

    def travel(way, distance, step, mode):
        chunk = table.at[mode, pl.ds(beside(-sign[way] * distance) * owned, owned)]
        return pltpu.make_async_remote_copy(
            src_ref=chunk,
            dst_ref=chunk,
            send_sem=ring_send,
            recv_sem=ring_recv.at[way, distance + step - 1, mode],
            device_id={"mem": beside(sign[way] * step)},
            device_id_type=MESH,
        )

    def arrival(way, distance, mode):
        chunk = table.at[mode, pl.ds(beside(-sign[way] * distance) * owned, owned)]
        return pltpu.make_async_remote_copy(
            src_ref=chunk,
            dst_ref=chunk,
            send_sem=ring_send,
            recv_sem=ring_recv.at[way, distance - 1, mode],
            device_id={"mem": beside(-sign[way])},
            device_id_type=MESH,
        )

    def relay(distance):
        for mode in range(3):
            for way in range(2):
                if 0 < distance <= reach[way]:
                    arrival(way, distance, mode).wait_recv()
                if distance + 2 <= reach[way]:
                    travel(way, distance, 2, mode).start()
        for mode in range(3):
            for way in range(2):
                if distance + 1 <= reach[way]:
                    travel(way, distance, 1, mode).start()

    relay(0)
    for copy in index_loads:
        copy.wait()

    live = live_ref[0, 0]
    wanted = [coords_ref[0, j] for j in range(slots)]

    def find(place, found):
        here = order_ref[0, place]
        return tuple(jnp.where(here == c, place, f) for c, f in zip(wanted, found))

    found = lax.fori_loop(0, groups * OWNED, find, (jnp.int32(0),) * slots, unroll=4)
    places = [jnp.where(j < live, found[j], -NONE) for j in range(slots)]
    code_row = lax.broadcasted_iota(jnp.int32, (8, HALF), 0)

    def send_to(buffer_out, buffer_in, send_sem, recv_sem, target):
        return pltpu.make_async_remote_copy(
            src_ref=buffer_out.at[target],
            dst_ref=buffer_in.at[group],
            send_sem=send_sem,
            recv_sem=recv_sem,
            device_id={"grp": target},
            device_id_type=MESH,
        )

    def wait_others(buffer, sem):
        others = buffer.at[pl.ds(0, groups - 1)]
        pltpu.make_async_copy(others, others, sem).wait()

    rows_set = (rows_out, rows_in, rows_send, rows_recv)
    code_set = (code_out, code_in, code_send, code_recv)

    def start_all(buffers):
        def one(step, carry):
            send_to(*buffers, lax.rem(group + step, groups)).start()
            return carry

        lax.fori_loop(1, groups, one, 0, unroll=True)

    def from_other(step):
        return lax.rem(group + groups - step, groups)

    def encode(owner, carry):
        low, high = jnp.int32(NONE), jnp.int32(-1)
        for j in range(slots):
            offset = places[j] - owner * OWNED
            mine = (offset >= 0) & (offset < OWNED)
            low = jnp.minimum(low, jnp.where(mine, offset, NONE))
            high = jnp.maximum(high, jnp.where(mine, offset, -1))
        high = jnp.where(high > low, high, NONE)
        lows[owner] = low
        highs[owner] = high
        code_out[owner] = jnp.where(code_row == 0, low, high)
        return carry

    lax.fori_loop(0, groups, encode, 0)
    start_all(code_set)

    for distance in range(2, reach[0], 2):
        relay(distance)
    gram_parts = {mode: (mode, 1) for mode in range(3)}

    def start_gram(start, count):
        def one(step, carry):
            target = lax.rem(group + step, groups)
            pltpu.make_async_remote_copy(
                src_ref=gram_out.at[target, pl.ds(start, count)],
                dst_ref=gram_in.at[group, pl.ds(start, count)],
                send_sem=gram_send,
                recv_sem=gram_recv,
                device_id={"grp": target},
                device_id_type=MESH,
            ).start()
            return carry

        lax.fori_loop(1, groups, one, 0, unroll=True)

    height = R // groups
    for mode in range(3):
        for distance in range(1, reach[0] + 1, 2):
            for way in range(2):
                if distance <= reach[way]:
                    arrival(way, distance, mode).wait_recv()
        if reach[0] % 2 == 0:
            arrival(0, reach[0], mode).wait_recv()
        factor = table[mode].reshape(owned * members * B, R)
        gram = lax.dot_general(
            factor, factor, (((0,), (0,)), ((), ())), preferred_element_type=jnp.float32
        )
        gram_out[:, mode] = gram.reshape(groups, height, R)
        if mode in gram_parts:
            start_gram(*gram_parts[mode])
    load.wait()

    def one_slot(j, carry):
        third = table[1, coords_ref[2, j]].astype(jnp.float32)
        fourth = table[2, coords_ref[3, j]].astype(jnp.float32)
        khatri = (third[:, None, :] * fourth[None, :, :]).reshape(B * B, R).astype(jnp.bfloat16)
        product = jnp.dot(blocks[j], khatri, preferred_element_type=jnp.float32)
        second = table[0, coords_ref[1, j]].astype(jnp.float32)
        parts[j] = jnp.sum(product.reshape(B, B, R) * second[None, :, :], axis=1)
        return carry

    lax.fori_loop(0, slots, one_slot, 0)

    def pack(owner, carry):
        values = [parts[j] for j in range(slots)]
        for slot, chosen in enumerate((lows[owner], highs[owner])):
            total = jnp.zeros((B, R), jnp.float32)
            for j in range(slots):
                total = total + jnp.where(places[j] - owner * OWNED == chosen, values[j], 0.0)
            rows_out[owner, slot] = total.astype(jnp.bfloat16)
        return carry

    lax.fori_loop(0, groups, pack, 0)

    wait_others(gram_in, gram_recv)

    def add_gram(step, total):
        return total + gram_in[from_other(step)]

    total = lax.fori_loop(1, groups, add_gram, gram_out[group], unroll=True)
    system[group] = total[0] * total[1] * total[2]

    def system_copy(index, target):
        return pltpu.make_async_remote_copy(
            src_ref=system.at[index],
            dst_ref=system.at[index],
            send_sem=system_send,
            recv_sem=system_recv,
            device_id={"grp": target},
            device_id_type=MESH,
        )

    def system_start(step, carry):
        system_copy(group, lax.rem(group + step, groups)).start()
        return carry

    lax.fori_loop(1, groups, system_start, 0, unroll=True)
    start_all(rows_set)

    passed = table.at[:, pl.ds(0, (reach[0] + reach[1]) * owned)]
    pltpu.make_async_copy(passed, passed, ring_send).wait()
    wait_others(gram_out, gram_send)
    wait_others(code_out, code_send)
    wait_others(system, system_recv)
    first_ref[...] = system[0 : groups // 2].reshape(HALF, R)[:, 0:HALF]
    invert_half(first_ref)
    first = first_ref[...]
    cross = system[0 : groups // 2].reshape(HALF, R)[:, HALF:R]
    weights = dot_full(first, cross)
    second_ref[...] = system[groups // 2 :].reshape(HALF, R)[:, HALF:R] - dot_full(
        cross, weights, 0, 0
    )
    def add_code(code, rows, totals):
        for slot in range(2):
            values = rows[slot].astype(jnp.float32)
            place = jnp.broadcast_to(code[slot : slot + 1], (B, HALF))
            place = jnp.concatenate([place, place], axis=1)
            totals = tuple(
                t + jnp.where(place == p, values, 0.0) for p, t in enumerate(totals)
            )
        return totals

    def add_rows(step, totals):
        source = from_other(step)
        return add_code(code_in[source], rows_in[source], totals)

    totals = (jnp.zeros((B, R), jnp.float32),) * OWNED
    totals = add_code(code_out[group], rows_out[group], totals)
    wait_others(code_in, code_recv)
    wait_others(rows_in, rows_recv)
    wait_others(system, system_send)
    wait_others(rows_out, rows_send)
    totals = lax.fori_loop(1, groups, add_rows, totals, unroll=4)
    sums = jnp.concatenate(totals, axis=0)
    left = sums[:, 0:HALF]
    right = sums[:, HALF:R] - dot_full(left, weights)
    left = dot_full(left, first)
    invert_half(second_ref)
    right = dot_full(right, second_ref[...])

    out_ref[:, HALF:R] = right
    out_ref[:, 0:HALF] = left - dot_full(right, weights, 1, 1)


def on_device(
    tensor_blocks, block_coords, live_count, owner_order, factor_two, factor_three, factor_four
):
    groups = lax.axis_size("grp")
    members = lax.axis_size("mem")
    slots = tensor_blocks.shape[0]
    owned = factor_two.shape[0] // B
    height = R // groups
    hbm = pl.BlockSpec(memory_space=pl.ANY)
    vmem = pl.BlockSpec(memory_space=pltpu.VMEM)
    dma = pltpu.SemaphoreType.DMA
    factors = [f.reshape(owned, B, R) for f in (factor_two, factor_three, factor_four)]
    solved = pl.pallas_call(
        functools.partial(update_kernel, groups, members),
        out_shape=jax.ShapeDtypeStruct((OWNED * B, R), jnp.float32),
        in_specs=[hbm] * 7,
        out_specs=vmem,
        scratch_shapes=[
            pltpu.SMEM(block_coords.shape, jnp.int32),
            pltpu.SMEM(live_count.shape, jnp.int32),
            pltpu.SMEM(owner_order.shape, jnp.int32),
            pltpu.VMEM(tensor_blocks.shape, jnp.bfloat16),
            pltpu.VMEM((3, members * owned, B, R), jnp.bfloat16),
            pltpu.VMEM((slots, B, R), jnp.float32),
            pltpu.VMEM((groups, 3, height, R), jnp.float32),
            pltpu.VMEM((groups, 3, height, R), jnp.float32),
            pltpu.VMEM((groups, height, R), jnp.float32),
            pltpu.VMEM((groups, 2, B, R), jnp.bfloat16),
            pltpu.VMEM((groups, 2, B, R), jnp.bfloat16),
            pltpu.VMEM((groups, 8, HALF), jnp.int32),
            pltpu.VMEM((groups, 8, HALF), jnp.int32),
            pltpu.SMEM((groups,), jnp.int32),
            pltpu.SMEM((groups,), jnp.int32),
            pltpu.VMEM((HALF, HALF), jnp.float32),
            pltpu.VMEM((HALF, HALF), jnp.float32),
            dma((7,)),
            dma,
            dma((2, members // 2, 3)),
        ]
        + [dma] * 8,
        compiler_params=pltpu.CompilerParams(
            collective_id=0, has_side_effects=True, vmem_limit_bytes=60 << 20
        ),
        name="update_rows",
    )(block_coords, live_count, owner_order, tensor_blocks, *factors)
    return solved[None]


def solution(mesh):
    return jax.shard_map(
        on_device,
        mesh=mesh,
        in_specs=(
            P(("grp", "mem"), None, None),
            P(None, ("grp", "mem")),
            P("grp", "mem"),
            P("mem", None),
            P(("grp", "mem"), None),
            P(("grp", "mem"), None),
            P(("grp", "mem"), None),
        ),
        out_specs=P("mem", "grp", None),
        check_vma=False,
    )
```
